256 devices in a mesh: dp: 8 (over x, core), tensor: 32 (over y, z).
Axes of the slice: x: 4, y: 4, z: 8, core: 2. Of those that a mesh axis runs over, the one named last changes fastest.
Arguments:
- features: bfloat16 [6144, 8192], P('dp', 'tensor'), parts along dimension 0, may hold values from -6 to 6
- token_adapter_index: int32 [6144], P('dp'), parts along dimension 0, may hold values from 0 to 63, as said below
- projection_weight: bfloat16 [8192, 8192], P('tensor'), may hold values from -0.125 to 0.125
- shrink_weight: bfloat16 [8192, 4096], P('tensor'), may hold values from -0.0625 to 0.0625
- expand_weight: bfloat16 [4096, 8192], P(None, 'tensor'), may hold values from -0.75 to 0.75
Outputs:
- projected: float32 [6144, 8192], P('dp', 'tensor'), parts along dimension 0
The draws below stay inside these ranges and needn't reach their ends.
There are 8 independent parts, one for each index of `dp`. The reference program is written for one: setup_inputs(seed, part) draws one part's arguments, and reference() takes and returns one part's arrays. A program takes and returns all parts, laid end to end along the dimension named above; an argument that names none is the same for every part. Nothing has to cross between parts.
Inputs may be any that keep to these rules, and one draw needn't show every extreme that they name: token_adapter_index never decreases along the tokens, so each adapter's tokens are contiguous; every adapter has 1 to 48 tokens, and one adapter has exactly 48.
All inputs are finite; a program needn't handle non-finite values.
Results may differ from the reference program's by a relative error of at most 0.0019.
Values may be sent and summed in bfloat16 or wider, within the bound.
A program may use at most 128 MiB of HBM per device.

```python
import jax
import jax.numpy as jnp

MODEL_WIDTH = 8192
ADAPTER_RANK = 64
ADAPTER_COUNT = 64
PROMPT_TOKENS = 768
MOST = 48


def segment_lengths(key):
    index = jnp.arange(ADAPTER_COUNT, dtype=jnp.int32)
    biggest = jax.random.randint(jax.random.fold_in(key, 11), (), 0, ADAPTER_COUNT)
    remaining = PROMPT_TOKENS - MOST
    share = remaining // (ADAPTER_COUNT - 1)
    leftover = remaining % (ADAPTER_COUNT - 1)
    ranking = index - (index > biggest).astype(jnp.int32)
    lengths = share + (ranking < leftover).astype(jnp.int32)
    lengths = jnp.where(index == biggest, MOST, lengths)
    order = jax.random.permutation(jax.random.fold_in(key, 12), ADAPTER_COUNT)
    first = order[0::2]
    second = order[1::2]
    moved = jax.random.randint(jax.random.fold_in(key, 13), (ADAPTER_COUNT // 2,), 0, share)
    moved = jnp.where((first == biggest) | (second == biggest), 0, moved)
    change = jnp.zeros((ADAPTER_COUNT,), jnp.int32).at[first].add(moved).at[second].add(-moved)
    return lengths + change


def draw_token_adapter_index(key, part):
    lengths = segment_lengths(key)
    ends = jnp.cumsum(lengths)
    positions = jnp.arange(PROMPT_TOKENS, dtype=jnp.int32)
    return jnp.sum((ends[None, :] <= positions[:, None]).astype(jnp.int32), axis=1).astype(jnp.int32)


def raised(array, key, source, target, shards_of, factor):
    def block_of(axis_at):
        return (jnp.arange(array.shape[axis_at]) // (array.shape[axis_at] // shards_of)).reshape((-1,) + (1,) * (array.ndim - 1 - axis_at))

    first = jax.random.permutation(key, shards_of)[block_of(target)]
    other_side = (block_of(target) + shards_of // 2) % shards_of
    return jnp.where((block_of(source) == first) | (block_of(source) == other_side), factor * array, array)


def level_of(rng, extent, split, low, largest):
    def one(position, parts):
        draws = jax.random.uniform(jax.random.fold_in(jax.random.fold_in(rng, 6), position), (parts,), jnp.float32, low / len(split), largest / len(split))
        return jnp.repeat(jnp.exp(draws), extent[position] // parts).reshape((-1,) + (1,) * (len(extent) - position - 1))

    level = one(*split[0])
    for cut in split[1:]:
        level = level * one(*cut)
    return level


def gaussian(stream_key, shape, scale, limit, cuts=(), kind=jnp.bfloat16):
    array = scale * jax.random.normal(stream_key, shape, jnp.float32)
    if cuts:
        array = array * level_of(stream_key, shape, cuts, -0.22, 0.18)
    return jnp.clip(array, -limit, limit).astype(kind)


def gaussian_with(own_key, extent, spread, limit, split, heavy, kind=jnp.bfloat16):
    drawn = spread * jax.random.normal(own_key, extent, jnp.float32)
    if split:
        drawn = drawn * level_of(own_key, extent, split, -0.22, 0.18)
    return jnp.clip(raised(drawn, jax.random.fold_in(own_key, 3), *heavy), -limit, limit).astype(kind)


def setup_inputs(seed: int = 0, part: int = 0) -> dict:
    key_list = jax.random.split(jax.random.key(seed), 6)
    part_splits = jax.random.split(jax.random.fold_in(key_list[5], part), 6)
    return {
        "features": gaussian(part_splits[0], (PROMPT_TOKENS, MODEL_WIDTH), 1.0, 6.0, ((1, 32),)),
        "token_adapter_index": draw_token_adapter_index(jax.random.fold_in(jax.random.fold_in(key_list[5], part), 71), part),
        "projection_weight": gaussian_with(key_list[2], (MODEL_WIDTH, MODEL_WIDTH), MODEL_WIDTH ** -0.5, 0.125, ((0, 32),), (0, 1, 32, 2.75)),
        "shrink_weight": gaussian(key_list[3], (MODEL_WIDTH, ADAPTER_COUNT * ADAPTER_RANK), MODEL_WIDTH ** -0.5, 0.0625, ((0, 32),)),
        "expand_weight": gaussian(key_list[4], (ADAPTER_COUNT * ADAPTER_RANK, MODEL_WIDTH), ADAPTER_RANK ** -0.5, 0.75, ((1, 32),)),
    }


def reference(features, token_adapter_index, projection_weight, shrink_weight, expand_weight):
    base_result = jnp.dot(features, projection_weight, preferred_element_type=jnp.float32)
    onehot = (token_adapter_index[:, None] == jnp.arange(ADAPTER_COUNT, dtype=jnp.int32)[None, :]).astype(jnp.float32)
    combined_output = jnp.dot(features, shrink_weight, preferred_element_type=jnp.float32).reshape(PROMPT_TOKENS, ADAPTER_COUNT, ADAPTER_RANK)
    shrink = jnp.einsum("tar,ta->tr", combined_output, onehot)
    shrunk = shrink.astype(jnp.bfloat16)
    widened_rank = (onehot.astype(jnp.bfloat16)[:, :, None] * shrunk[:, None, :]).reshape(PROMPT_TOKENS, ADAPTER_COUNT * ADAPTER_RANK)
    lowrank_delta = jnp.dot(widened_rank, expand_weight, preferred_element_type=jnp.float32)
    return base_result + lowrank_delta
```

```python
import jax
import jax.numpy as jnp
from jax import lax
from jax.experimental import pallas as pl
from jax.experimental.pallas import tpu as pltpu
from jax.sharding import PartitionSpec as P

ADAPTER_RANK = 64
NX, NC, NY, NZ = 4, 2, 4, 8
ROWS, KD, COLS = 768, 256, 256
NB = 6
BR = ROWS // NB
HOPS = (3, 4)
KORD = (0, 1, 7, 2, 6, 3, 5, 4)
SLOT = {k: s for s, k in enumerate(KORD)}
GROUPS = ((0, 1), (1, 2), (3, 2), (5, 2), (7, 1))
HALF = KD // NC
QUART = HALF // 2


def base_kernel(
    f_ref, w_ref, o_ref, fg, wg, ys, yr,
    loc, wzs, wzr, wxs, wxr, wrs, wrr, wcs, wcr, fs, fr, yss, yrs,
):
    dp, tensor = lax.axis_index("dp"), lax.axis_index("tensor")
    x, c = dp // NC, dp % NC
    y, z = tensor // NZ, tensor % NZ

    def at_z(k):
        return {"tensor": y * NZ + (z + k) % NZ}

    def at_y(d):
        return {"tensor": ((y + d) % NY) * NZ + z}

    def at_x(d):
        return {"dp": ((x + d) % NX) * NC + c}

    sibling = {"dp": x * NC + (1 - c)}

    own_f = pltpu.make_async_copy(f_ref, fg.at[0], loc.at[0])
    own_f.start()

    def w_part(zz):
        return w_ref.at[
            pl.ds(pl.multiple_of(c * HALF, HALF), HALF),
            pl.ds(pl.multiple_of((x * NZ + zz) * COLS, COLS), COLS),
        ]

    half = pl.ds(pl.multiple_of(c * HALF, HALF), HALF)
    own_w = pltpu.make_async_copy(w_part(z), wg.at[x, 0, half], loc.at[1])
    own_w.start()

    peers = (
        [at_z(k) for k in range(1, NZ)]
        + [at_y(d) for d in range(1, NY)]
        + [at_x(1), at_x(-1 + NX), sibling]
    )
    barrier = pltpu.get_barrier_semaphore()
    for peer in peers:
        pl.semaphore_signal(barrier, inc=1, device_id=peer, device_id_type=pl.DeviceIdType.MESH)
    pl.semaphore_wait(barrier, len(peers))

    def remote(src, dst, s, r, dev):
        return pltpu.make_async_remote_copy(
            src_ref=src, dst_ref=dst, send_sem=s, recv_sem=r,
            device_id=dev, device_id_type=pl.DeviceIdType.MESH,
        )

    def wz(k):
        return remote(
            w_part((z + k) % NZ), wg.at[x, SLOT[k], half], wzs.at[k - 1], wzr.at[k - 1], at_z(k)
        )

    def wx(d, g, owner):
        s0, n = GROUPS[g]
        part = wg.at[owner, pl.ds(s0, n), half]
        return remote(part, part, wxs.at[d, g], wxr.at[d, g], at_x(1 if d == 0 else NX - 1))

    def wr(d, g, owner):
        s0, n = GROUPS[g]
        rows = pl.ds(pl.multiple_of(c * HALF + d * QUART, QUART), QUART)
        part = wg.at[owner, pl.ds(s0, n), rows]
        return remote(part, part, wrs.at[d, g], wrr.at[d, g], at_x(1 if d == 0 else NX - 1))

    def wc(i, h, which):
        owner = (x + (0, NX - 1, 1, 2)[i]) % NX
        part = wg.at[owner, pl.ds(4 * h, 4), pl.ds(pl.multiple_of(which * HALF, HALF), HALF)]
        return remote(part, part, wcs.at[i, h], wcr.at[i, h], sibling)

    def fc(d, h, b):
        src = SLOT[h] if d == 0 else SLOT[(NZ - h) % NZ]
        dst = SLOT[h + 1] if d == 0 else SLOT[NZ - 1 - h]
        rows = pl.ds(b * BR if isinstance(b, int) else pl.multiple_of(b * BR, BR), BR)
        return remote(
            fg.at[src, rows], fg.at[dst, rows], fs.at[d, h, b], fr.at[d, h, b],
            at_z(1 if d == 0 else NZ - 1),
        )

    def yc(d, b):
        rows = pl.ds(b * BR if isinstance(b, int) else pl.multiple_of(b * BR, BR), BR)
        return remote(ys.at[d - 1, rows], yr.at[d - 1, rows], yss.at[d - 1, b], yrs.at[d - 1, b], at_y(d))

    for k in KORD[1:]:
        wz(k).start()
    own_w.wait()
    wx(0, 0, x).start()
    wx(1, 0, x).start()
    own_f.wait()
    fc(0, 0, 0).start()
    fc(1, 0, 0).start()
    for g in range(1, len(GROUPS)):
        s0, n = GROUPS[g]
        for s in range(s0, s0 + n):
            wz(KORD[s]).wait_recv()
        wx(0, g, x).start()
        wx(1, g, x).start()
        if g == 2:
            wc(0, 0, c).start()
    wc(0, 1, c).start()

    left, right = (x + NX - 1) % NX, (x + 1) % NX

    def from_x(g):
        wx(0, g, left).wait_recv()
        wr(0, g, left).start()
        wx(1, g, right).wait_recv()
        wr(1, g, right).start()

    def from_relay(g):
        wr(0, g, (x + 2) % NX).wait_recv()
        wr(1, g, (x + 2) % NX).wait_recv()

    def forward(t, static):
        def when(cond, fn):
            if static:
                if cond:
                    fn()
            else:
                pl.when(cond)(fn)

        def own():
            fc(0, 0, t).start()
            fc(1, 0, t).start()

        when(t < NB, own)
        for h in range(max(HOPS), 0, -1):
            def hop(h=h):
                for d in range(2):
                    if h <= HOPS[d]:
                        fc(d, h - 1, t - h).wait_recv()
                        if h < HOPS[d]:
                            fc(d, h, t - h).start()

            when((t - h >= 0) & (t - h < NB), hop)

    def compute(b):
        rows = pl.ds(pl.multiple_of(b * BR, BR), BR)
        lhs = jnp.concatenate([fg[s, rows, :] for s in range(NZ)], axis=1)
        for d in (2, 1, 3, 0):
            acc = jnp.dot(
                lhs, wg[(y + d) % NY].reshape(NZ * KD, COLS), preferred_element_type=jnp.float32
            )
            if d == 0:
                o_ref[rows, :] = acc
            else:
                ys[d - 1, rows, :] = acc.astype(jnp.bfloat16)
                yc(d, b).start()

    def finish(b):
        rows = pl.ds(pl.multiple_of(b * BR, BR), BR)
        total = o_ref[rows, :]
        for d in (1, 3, 2):
            yc(d, b).wait_recv()
            total = total + yr[d - 1, rows, :].astype(jnp.float32)
        o_ref[rows, :] = total

    forward(1, True)
    from_x(0)
    from_x(1)
    forward(2, True)
    from_x(2)
    wc(1, 0, c).start()
    wc(2, 0, c).start()
    from_relay(0)
    from_relay(1)
    forward(3, True)
    from_x(3)
    from_x(4)
    wc(1, 1, c).start()
    wc(2, 1, c).start()
    from_relay(2)
    from_relay(3)
    wc(3, 0, c).start()
    from_relay(4)
    wc(3, 1, c).start()
    for h in range(2):
        for i in range(4):
            wc(i, h, 1 - c).wait_recv()

    def tick(t, carry):
        forward(t, False)
        compute(t - 4)

        @pl.when(t > 4)
        def _():
            finish(t - 5)

        return carry

    lax.fori_loop(4, NB + 4, tick, 0)
    finish(NB - 1)

    for k in range(1, NZ):
        wz(k).wait_send()
    for d in range(2):
        for g in range(len(GROUPS)):
            wx(d, g, x).wait_send()
            wr(d, g, x).wait_send()
    for i in range(4):
        for h in range(2):
            wc(i, h, c).wait_send()

    def drain(b, carry):
        for d in range(2):
            for h in range(HOPS[d]):
                fc(d, h, b).wait_send()
        for d in range(1, NY):
            yc(d, b).wait_send()
        return carry

    lax.fori_loop(0, NB, drain, 0)


def base_product(features, projection_weight):
    dma = pltpu.SemaphoreType.DMA
    return pl.pallas_call(
        base_kernel,
        out_shape=jax.ShapeDtypeStruct((ROWS, COLS), jnp.float32),
        in_specs=[pl.BlockSpec(memory_space=pl.ANY)] * 2,
        out_specs=pl.BlockSpec(memory_space=pltpu.VMEM),
        scratch_shapes=[
            pltpu.VMEM((NZ, ROWS, KD), jnp.bfloat16),
            pltpu.VMEM((NX, NZ, KD, COLS), jnp.bfloat16),
            pltpu.VMEM((NY - 1, ROWS, COLS), jnp.bfloat16),
            pltpu.VMEM((NY - 1, ROWS, COLS), jnp.bfloat16),
            dma((2,)),
            dma((NZ - 1,)), dma((NZ - 1,)),
            dma((2, len(GROUPS))), dma((2, len(GROUPS))),
            dma((2, len(GROUPS))), dma((2, len(GROUPS))),
            dma((4, 2)), dma((4, 2)),
            dma((2, 4, NB)), dma((2, 4, NB)),
            dma((NY - 1, NB)), dma((NY - 1, NB)),
        ],
        compiler_params=pltpu.CompilerParams(
            collective_id=0, has_side_effects=True, vmem_limit_bytes=40 * 1024 * 1024
        ),
        cost_estimate=pl.CostEstimate(
            flops=2 * ROWS * NZ * KD * NY * COLS, bytes_accessed=16 * 1024 * 1024, transcendentals=0
        ),
    )(features, projection_weight)


def on_device(features, token_adapter_index, projection_weight, shrink_weight, expand_weight):
    rows = features.shape[0]
    rank_column_values = shrink_weight.shape[1]
    rank = ADAPTER_RANK
    adapters = rank_column_values // rank
    onehot = token_adapter_index[:, None] == jnp.arange(adapters, dtype=jnp.int32)[None, :]
    combined_output = jnp.dot(features, shrink_weight, preferred_element_type=jnp.float32).reshape(
        rows, adapters, rank
    )
    partial_shrink = jnp.sum(jnp.where(onehot[:, :, None], combined_output, 0.0), axis=1)
    shrink = lax.psum(partial_shrink, "tensor")
    shrunk = shrink.astype(jnp.bfloat16)
    widened_rank = (onehot.astype(jnp.bfloat16)[:, :, None] * shrunk[:, None, :]).reshape(
        rows, rank_column_values
    )
    lowrank_delta = jnp.dot(widened_rank, expand_weight, preferred_element_type=jnp.float32)
    return base_product(features, projection_weight) + lowrank_delta


def solution(mesh):
    in_specs = (P("dp", "tensor"), P("dp"), P("tensor", None), P("tensor", None), P(None, "tensor"))
    out_specs = P("dp", "tensor")
    return jax.shard_map(
        on_device, mesh=mesh, in_specs=in_specs, out_specs=out_specs, check_vma=False
    )
```

```python
import jax
import jax.numpy as jnp
from jax import lax
from jax.experimental import pallas as pl
from jax.experimental.pallas import tpu as pltpu
from jax.sharding import PartitionSpec as P

ADAPTER_RANK = 64
NX, NC, NY, NZ = 4, 2, 4, 8
ROWS, KD, COLS = 768, 256, 256
RANKS = 4096
PACKED = ROWS // 2
PY = PACKED // NY
PZ = 16
ZS = PY // PZ
CHUNKS = ((0, 128), (128, 128), (256, 128), (384, 128), (512, 128), (640, 128))
NB = len(CHUNKS)


def hops(d, b):
    return 3 + (b + d) % 2


KORD = (0, 1, 7, 2, 6, 3, 5, 4)
SLOT = {k: s for s, k in enumerate(KORD)}
GROUPS = ((0, 1), (1, 2), (3, 2), (5, 2), (7, 1))
GROUP_OF = {KORD[s]: g for g, (s0, n) in enumerate(GROUPS) for s in range(s0, s0 + n)}
HALF = KD // NC
QUART = HALF // 2
def kernel(
    f_ref, i_ref, w_ref, s_ref, e_ref, o_ref,
    fg, wg, ys, yr, sv, ev, idx, acc128, packed, fromy, part, fromz, shb, shr,
    loc, wzs, wzr, wxs, wxr, wrs, wrr, wcs, wcr, fs, fr, yss, yrs,
    ls, lr,
):
    dp, tensor = lax.axis_index("dp"), lax.axis_index("tensor")
    x, c = dp // NC, dp % NC
    y, z = tensor // NZ, tensor % NZ

    def at_z(k):
        return {"tensor": y * NZ + (z + k) % NZ}

    def at_y(d):
        return {"tensor": ((y + d) % NY) * NZ + z}

    def at_x(d):
        return {"dp": ((x + d) % NX) * NC + c}

    sibling = {"dp": x * NC + (1 - c)}

    own_f = pltpu.make_async_copy(f_ref, fg.at[0], loc.at[0])
    own_f.start()

    def w_part(zz):
        return w_ref.at[
            pl.ds(pl.multiple_of(c * HALF, HALF), HALF),
            pl.ds(pl.multiple_of((x * NZ + zz) * COLS, COLS), COLS),
        ]

    half = pl.ds(pl.multiple_of(c * HALF, HALF), HALF)
    own_w = pltpu.make_async_copy(w_part(z), wg.at[x, 0, half], loc.at[1])
    own_w.start()

    own_s = pltpu.make_async_copy(s_ref, sv, loc.at[2])
    own_s.start()
    own_e = pltpu.make_async_copy(e_ref, ev, loc.at[3])
    own_e.start()

    peers = (
        [at_z(k) for k in range(1, NZ)]
        + [at_y(d) for d in range(1, NY)]
        + [at_x(1), at_x(-1 + NX), sibling]
    )
    barrier = pltpu.get_barrier_semaphore()
    for peer in peers:
        pl.semaphore_signal(barrier, inc=1, device_id=peer, device_id_type=pl.DeviceIdType.MESH)
    pl.semaphore_wait(barrier, len(peers))

    def remote(src, dst, s, r, dev):
        return pltpu.make_async_remote_copy(
            src_ref=src, dst_ref=dst, send_sem=s, recv_sem=r,
            device_id=dev, device_id_type=pl.DeviceIdType.MESH,
        )

    def wz(k):
        return remote(
            w_part((z + k) % NZ), wg.at[x, SLOT[k], half], wzs.at[0], wzr.at[GROUP_OF[k]], at_z(k)
        )

    def wx(d, g, owner):
        s0, n = GROUPS[g]
        part = wg.at[owner, pl.ds(s0, n), half]
        return remote(part, part, wxs.at[0], wxr.at[d, g], at_x(1 if d == 0 else NX - 1))

    def wr(d, g, owner):
        s0, n = GROUPS[g]
        rows = pl.ds(pl.multiple_of(c * HALF + d * QUART, QUART), QUART)
        part = wg.at[owner, pl.ds(s0, n), rows]
        return remote(part, part, wrs.at[0], wrr.at[g], at_x(1 if d == 0 else NX - 1))

    def wc(i, h, which):
        owner = (x + (0, NX - 1, 1, 2)[i]) % NX
        part = wg.at[owner, pl.ds(4 * h, 4), pl.ds(pl.multiple_of(which * HALF, HALF), HALF)]
        return remote(part, part, wcs.at[0], wcr.at[0], sibling)

    def rows_of(b):
        return pl.ds(*CHUNKS[b])

    def fc(d, h, b):
        src = SLOT[h] if d == 0 else SLOT[(NZ - h) % NZ]
        dst = SLOT[h + 1] if d == 0 else SLOT[NZ - 1 - h]
        rows = rows_of(b)
        return remote(
            fg.at[src, rows], fg.at[dst, rows], fs.at[0], fr.at[d, h, b], at_z(1 if d == 0 else NZ - 1)
        )

    def yc(d, b):
        rows = rows_of(b)
        return remote(ys.at[d - 1, rows], yr.at[d - 1, rows], yss.at[0], yrs.at[b], at_y(d))

    def sent(ref, sem):
        remote(ref, ref, sem, sem, sibling).wait_send()

    def received(ref, sem):
        remote(ref, ref, sem, sem, sibling).wait_recv()

    def l1(d):
        rows = pl.ds(pl.multiple_of(((y + d) % NY) * PY, PY), PY)
        return remote(packed.at[rows], fromy.at[d - 1], ls.at[0], lr.at[0], at_y(d))

    def l2(k):
        rows = pl.ds(pl.multiple_of(((z + k) % NZ) * PZ, PZ), PZ)
        return remote(part.at[rows], fromz.at[k - 1], ls.at[1], lr.at[1], at_z(k))

    def l3(k, source):
        piece = shb.at[pl.ds(pl.multiple_of(y * PY + source * PZ, PZ), PZ)]
        return remote(piece, piece, ls.at[2], lr.at[2], at_z(k))

    def l4(d, source):
        piece = shb.at[pl.ds(pl.multiple_of(source * PY, PY), PY)]
        return remote(piece, piece, ls.at[3], lr.at[3], at_y(d))

    def adapters_of_tokens():
        eye = lax.broadcasted_iota(jnp.int32, (128, 128), 0) == lax.broadcasted_iota(
            jnp.int32, (128, 128), 1
        )
        upper = (lax.broadcasted_iota(jnp.int32, (128, 128), 1) >= ADAPTER_RANK).astype(jnp.float32)
        ones = jnp.ones((128, 128), jnp.bfloat16)
        for i in range(ROWS // 128):
            row = jnp.broadcast_to(i_ref[pl.ds(i, 1), :].astype(jnp.float32), (128, 128))
            diagonal = jnp.where(eye, row, 0.0).astype(jnp.bfloat16)
            spread = jnp.dot(diagonal, ones, preferred_element_type=jnp.float32)
            idx[pl.ds(i * 128, 128), :] = spread - upper
        acc128[...] = jnp.zeros_like(acc128)

    def shrink_columns(j, carry):
        columns = sv[:, pl.ds(pl.multiple_of(j * 256, 256), 256)]
        first = (4 * j).astype(jnp.float32)
        for r in range(3):
            rows = pl.ds(r * 256, 256)
            out = jnp.dot(fg[0, rows, :], columns, preferred_element_type=jnp.float32)
            which = idx[rows, :]
            acc128[rows, :] += jnp.where(which == first, out[:, :128], 0.0) + jnp.where(
                which == first + 2.0, out[:, 128:], 0.0
            )
        return carry

    def shrink_part(i):
        lax.fori_loop(4 * i, 4 * i + 4, shrink_columns, 0)

    lower = lax.broadcasted_iota(jnp.int32, (96, 128), 1) < ADAPTER_RANK

    def shrink_to_y():
        for r in range(PACKED // 96):
            a = acc128[pl.ds(r * 96, 96), :]
            b = acc128[pl.ds(PACKED + r * 96, 96), :]
            packed[pl.ds(r * 96, 96), :] = jnp.where(
                lower, a + pltpu.roll(a, ADAPTER_RANK, 1), b + pltpu.roll(b, ADAPTER_RANK, 1)
            )
        for d in (2, 1, 3):
            l1(d).start()

    def shrink_to_z():
        received(fromy, lr.at[0])
        part[...] = (
            packed[pl.ds(pl.multiple_of(y * PY, PY), PY), :] + fromy[0] + fromy[1] + fromy[2]
        )
        for k in range(1, NZ):
            @pl.when((z + k) % NZ < ZS)
            def _(k=k):
                l2(k).start()

    def shrunk_to_z():
        @pl.when(z < ZS)
        def _():
            total = part[pl.ds(pl.multiple_of(z * PZ, PZ), PZ), :]
            received(fromz, lr.at[1])
            for k in range(1, NZ):
                total = total + fromz[k - 1]
            shb[pl.ds(pl.multiple_of(y * PY + z * PZ, PZ), PZ), :] = total.astype(jnp.bfloat16)
            for k in range(1, NZ):
                l3(k, z).start()

    def shrunk_to_y():
        @pl.when(z < ZS)
        def _():
            received(shb.at[pl.ds(0, (ZS - 1) * PZ)], lr.at[2])

        @pl.when(z >= ZS)
        def _():
            received(shb.at[pl.ds(0, ZS * PZ)], lr.at[2])

        for d in (2, 1, 3):
            l4(d, y).start()

    def shrunk_here():
        received(shb.at[pl.ds(0, (NY - 1) * PY)], lr.at[3])
        for r in range(PACKED // 96):
            a = shb[pl.ds(r * 96, 96), :].astype(jnp.float32)
            b = pltpu.roll(a, ADAPTER_RANK, 1)
            shr[pl.ds(r * 96, 96), :] = jnp.where(lower, a, b)
            shr[pl.ds(PACKED + r * 96, 96), :] = jnp.where(lower, b, a)

    def expand(b):
        rows, n = rows_of(b), CHUNKS[b][1]
        which, values = idx[rows, :], shr[rows, :]

        def step(j, total):
            first = (8 * j).astype(jnp.float32)
            wide = jnp.concatenate(
                [jnp.where(which == first + 2.0 * i, values, 0.0).astype(jnp.bfloat16) for i in range(4)],
                axis=1,
            )
            return total + jnp.dot(
                wide, ev[pl.ds(pl.multiple_of(j * 512, 512), 512), :], preferred_element_type=jnp.float32
            )

        o_ref[rows, :] += lax.fori_loop(0, RANKS // 512, step, jnp.zeros((n, COLS), jnp.float32))

    left, right = (x + NX - 1) % NX, (x + 1) % NX

    def from_x(g):
        wx(0, g, left).wait_recv()
        wr(0, g, left).start()
        wx(1, g, right).wait_recv()
        wr(1, g, right).start()

    def from_relay(g):
        s0, n = GROUPS[g]
        received(wg.at[(x + 2) % NX, pl.ds(s0, n), half], wrr.at[g])

    def own(b):
        for d in range(2):
            fc(d, 0, b).start()

    def pass_on(h, b):
        for d in range(2):
            if h <= hops(d, b):
                fc(d, h - 1, b).wait_recv()
            if h < hops(d, b):
                fc(d, h, b).start()

    def from_z(g):
        s0, n = GROUPS[g]
        received(wg.at[x, pl.ds(s0, n), half], wzr.at[g])
        wx(0, g, x).start()
        wx(1, g, x).start()

    def weight_to_z():
        for k in KORD[1:]:
            wz(k).start()
        own_w.wait()
        wx(0, 0, x).start()
        wx(1, 0, x).start()

    def shrink_start():
        adapters_of_tokens()
        own_s.wait()

    def weights_here():
        other = pl.ds(pl.multiple_of((1 - c) * HALF, HALF), HALF)
        received(wg.at[pl.ds(0, NX), pl.ds(0, NZ), other], wcr.at[0])

    def expand_here():
        own_e.wait()
        shrunk_here()

    def product(b):
        rows = rows_of(b)
        lhs = jnp.concatenate([fg[s, rows, :] for s in range(NZ)], axis=1)
        for d in (2, 1, 3, 0):
            acc = jnp.dot(
                lhs, wg[(y + d) % NY].reshape(NZ * KD, COLS), preferred_element_type=jnp.float32
            )
            if d == 0:
                o_ref[rows, :] = acc
            else:
                ys[d - 1, rows, :] = acc.astype(jnp.bfloat16)
                yc(d, b).start()

    def finish(b):
        rows = rows_of(b)
        received(yr.at[pl.ds(0, NY - 1), rows], yrs.at[b])
        total = o_ref[rows, :]
        for d in (1, 3, 2):
            total = total + yr[d - 1, rows, :].astype(jnp.float32)
        o_ref[rows, :] = total

    own_f.wait()
    weight_to_z()
    own(0)
    own(1)
    shrink_start()
    shrink_part(0)
    shrink_part(1)
    shrink_part(2)
    shrink_part(3)
    shrink_to_y()
    from_z(1)
    from_x(0)
    pass_on(1, 0)
    pass_on(1, 1)
    own(2)
    own(3)
    from_z(2)
    wc(0, 0, c).start()
    from_x(1)
    shrink_to_z()
    pass_on(2, 0)
    pass_on(2, 1)
    pass_on(1, 2)
    pass_on(1, 3)
    from_z(3)
    from_relay(0)
    from_x(2)
    shrunk_to_z()
    from_z(4)
    wc(0, 1, c).start()
    pass_on(3, 0)
    pass_on(3, 1)
    own(4)
    own(5)
    from_relay(1)
    wc(1, 0, c).start()
    wc(2, 0, c).start()
    from_x(3)
    from_x(4)
    shrunk_to_y()
    pass_on(2, 2)
    pass_on(2, 3)
    wc(1, 1, c).start()
    wc(2, 1, c).start()
    from_relay(2)
    from_relay(3)
    wc(3, 0, c).start()
    pass_on(1, 4)
    pass_on(1, 5)
    from_relay(4)
    wc(3, 1, c).start()
    weights_here()
    pass_on(4, 0)
    pass_on(4, 1)
    product(0)
    product(1)
    pass_on(3, 2)
    pass_on(3, 3)
    expand_here()
    pass_on(2, 4)
    pass_on(2, 5)
    expand(0)
    pass_on(4, 2)
    product(2)
    pass_on(4, 3)
    product(3)
    pass_on(3, 4)
    pass_on(3, 5)
    expand(1)
    pass_on(4, 4)
    product(4)
    pass_on(4, 5)
    product(5)
    expand(2)
    expand(3)
    expand(4)
    expand(5)
    finish(0)
    finish(1)
    finish(2)
    finish(3)
    finish(4)
    finish(5)

    sent(wg.at[0, pl.ds(0, NZ - 1), pl.ds(0, HALF)], wzs.at[0])
    sent(wg.at[pl.ds(0, 2), pl.ds(0, NZ), pl.ds(0, HALF)], wxs.at[0])
    sent(wg.at[0, pl.ds(0, NZ), pl.ds(0, HALF)], wrs.at[0])
    sent(wg.at[pl.ds(0, NX), pl.ds(0, NZ), pl.ds(0, HALF)], wcs.at[0])
    sent(fg.at[pl.ds(0, NZ - 1)], fs.at[0])
    sent(ys, yss.at[0])
    sent(fromy, ls.at[0])

    @pl.when(z < ZS)
    def _():
        sent(part.at[pl.ds(0, (ZS - 1) * PZ)], ls.at[1])
        sent(shb.at[pl.ds(0, (NZ - 1) * PZ)], ls.at[2])

    @pl.when(z >= ZS)
    def _():
        sent(part.at[pl.ds(0, ZS * PZ)], ls.at[1])

    sent(shb.at[pl.ds(0, (NY - 1) * PY)], ls.at[3])


def on_device(features, token_adapter_index, projection_weight, shrink_weight, expand_weight):
    dma = pltpu.SemaphoreType.DMA
    anywhere = pl.BlockSpec(memory_space=pltpu.HBM)
    vmem = pl.BlockSpec(memory_space=pltpu.VMEM)
    return pl.pallas_call(
        kernel,
        out_shape=jax.ShapeDtypeStruct((ROWS, COLS), jnp.float32),
        in_specs=[anywhere, vmem, anywhere, anywhere, anywhere],
        out_specs=vmem,
        scratch_shapes=[
            pltpu.VMEM((NZ, ROWS, KD), jnp.bfloat16),
            pltpu.VMEM((NX, NZ, KD, COLS), jnp.bfloat16),
            pltpu.VMEM((NY - 1, ROWS, COLS), jnp.bfloat16),
            pltpu.VMEM((NY - 1, ROWS, COLS), jnp.bfloat16),
            pltpu.VMEM((KD, RANKS), jnp.bfloat16),
            pltpu.VMEM((RANKS, COLS), jnp.bfloat16),
            pltpu.VMEM((ROWS, 128), jnp.float32),
            pltpu.VMEM((ROWS, 128), jnp.float32),
            pltpu.VMEM((PACKED, 128), jnp.float32),
            pltpu.VMEM((NY - 1, PY, 128), jnp.float32),
            pltpu.VMEM((PY, 128), jnp.float32),
            pltpu.VMEM((NZ - 1, PZ, 128), jnp.float32),
            pltpu.VMEM((PACKED, 128), jnp.bfloat16),
            pltpu.VMEM((ROWS, 128), jnp.float32),
            dma((4,)),
            dma((1,)), dma((len(GROUPS),)),
            dma((1,)), dma((2, len(GROUPS))),
            dma((1,)), dma((len(GROUPS),)),
            dma((1,)), dma((1,)),
            dma((1,)), dma((2, 4, NB)),
            dma((1,)), dma((NB,)),
            dma((4,)), dma((4,)),
        ],
        compiler_params=pltpu.CompilerParams(
            collective_id=0, has_side_effects=True, vmem_limit_bytes=62 * 1024 * 1024
        ),
        cost_estimate=pl.CostEstimate(
            flops=2 * ROWS * (NZ * KD * NY * COLS + 2 * KD * RANKS),
            bytes_accessed=16 * 1024 * 1024,
            transcendentals=0,
        ),
    )(
        features,
        token_adapter_index.reshape(ROWS // 128, 128),
        projection_weight,
        shrink_weight,
        expand_weight,
    )


def solution(mesh):
    in_specs = (P("dp", "tensor"), P("dp"), P("tensor", None), P("tensor", None), P(None, "tensor"))
    out_specs = P("dp", "tensor")
    return jax.shard_map(
        on_device, mesh=mesh, in_specs=in_specs, out_specs=out_specs, check_vma=False
    )
```

```python
import jax
import jax.numpy as jnp
from jax import lax
from jax.experimental import pallas as pl
from jax.experimental.pallas import tpu as pltpu
from jax.sharding import PartitionSpec as P

ADAPTER_RANK = 64
NX, NC, NY, NZ = 4, 2, 4, 8
ROWS, KD, COLS = 768, 256, 256
RANKS = 4096
PACKED = ROWS // 2
PY = PACKED // NY
PZ = 16
ZS = PY // PZ
CHUNKS = ((0, 128), (128, 128), (256, 128), (384, 128), (512, 128), (640, 128))
NB = len(CHUNKS)


def hops(d, b):
    return 3 + (b + d) % 2


KORD = (0, 1, 7, 2, 6, 3, 5, 4)
SLOT = {k: s for s, k in enumerate(KORD)}
GROUPS = ((0, 1), (1, 2), (3, 2), (5, 2), (7, 1))
GROUP_OF = {KORD[s]: g for g, (s0, n) in enumerate(GROUPS) for s in range(s0, s0 + n)}
HALF = KD // NC
QUART = HALF // 2
def kernel(
    f_ref, i_ref, w_ref, s_ref, e_ref, o_ref,
    fg, wg, ys, yr, sv, ev, idx, acc, acc128, packed, fromy, part, fromz, shb, shr,
    loc, wzs, wzr, wxs, wxr, wrs, wrr, wcs, wcr, fs, fr, yss, yrs,
    ls, lr,
):
    dp, tensor = lax.axis_index("dp"), lax.axis_index("tensor")
    x, c = dp // NC, dp % NC
    y, z = tensor // NZ, tensor % NZ

    def at_z(k):
        return {"tensor": y * NZ + (z + k) % NZ}

    def at_y(d):
        return {"tensor": ((y + d) % NY) * NZ + z}

    def at_x(d):
        return {"dp": ((x + d) % NX) * NC + c}

    sibling = {"dp": x * NC + (1 - c)}

    own_f = pltpu.make_async_copy(f_ref, fg.at[0], loc.at[0])
    own_f.start()

    def w_part(zz):
        return w_ref.at[
            pl.ds(pl.multiple_of(c * HALF, HALF), HALF),
            pl.ds(pl.multiple_of((x * NZ + zz) * COLS, COLS), COLS),
        ]

    half = pl.ds(pl.multiple_of(c * HALF, HALF), HALF)
    own_w = pltpu.make_async_copy(w_part(z), wg.at[x, 0, half], loc.at[1])
    own_w.start()

    own_s = pltpu.make_async_copy(s_ref, sv, loc.at[2])
    own_s.start()
    own_e = pltpu.make_async_copy(e_ref, ev, loc.at[3])
    own_e.start()

    peers = (
        [at_z(k) for k in range(1, NZ)]
        + [at_y(d) for d in range(1, NY)]
        + [at_x(1), at_x(-1 + NX), sibling]
    )
    barrier = pltpu.get_barrier_semaphore()
    for peer in peers:
        pl.semaphore_signal(barrier, inc=1, device_id=peer, device_id_type=pl.DeviceIdType.MESH)
    pl.semaphore_wait(barrier, len(peers))

    def remote(src, dst, s, r, dev):
        return pltpu.make_async_remote_copy(
            src_ref=src, dst_ref=dst, send_sem=s, recv_sem=r,
            device_id=dev, device_id_type=pl.DeviceIdType.MESH,
        )

    def wz(k):
        return remote(
            w_part((z + k) % NZ), wg.at[x, SLOT[k], half], wzs.at[0], wzr.at[GROUP_OF[k]], at_z(k)
        )

    def wx(d, g, owner):
        s0, n = GROUPS[g]
        part = wg.at[owner, pl.ds(s0, n), half]
        return remote(part, part, wxs.at[0], wxr.at[d, g], at_x(1 if d == 0 else NX - 1))

    def wr(d, g, owner):
        s0, n = GROUPS[g]
        rows = pl.ds(pl.multiple_of(c * HALF + d * QUART, QUART), QUART)
        part = wg.at[owner, pl.ds(s0, n), rows]
        return remote(part, part, wrs.at[0], wrr.at[g], at_x(1 if d == 0 else NX - 1))

    def wc(i, h, which):
        owner = (x + (0, NX - 1, 1, 2)[i]) % NX
        part = wg.at[owner, pl.ds(4 * h, 4), pl.ds(pl.multiple_of(which * HALF, HALF), HALF)]
        return remote(part, part, wcs.at[0], wcr.at[0], sibling)

    def rows_of(b):
        return pl.ds(*CHUNKS[b])

    def fc(d, h, b):
        src = SLOT[h] if d == 0 else SLOT[(NZ - h) % NZ]
        dst = SLOT[h + 1] if d == 0 else SLOT[NZ - 1 - h]
        rows = rows_of(b)
        return remote(
            fg.at[src, rows], fg.at[dst, rows], fs.at[0], fr.at[d, h, b], at_z(1 if d == 0 else NZ - 1)
        )

    def yc(d, b):
        rows = rows_of(b)
        return remote(ys.at[d - 1, rows], yr.at[d - 1, rows], yss.at[0], yrs.at[b], at_y(d))

    def sent(ref, sem):
        remote(ref, ref, sem, sem, sibling).wait_send()

    def received(ref, sem):
        remote(ref, ref, sem, sem, sibling).wait_recv()

    def l1(d):
        rows = pl.ds(pl.multiple_of(((y + d) % NY) * PY, PY), PY)
        return remote(packed.at[rows], fromy.at[d - 1], ls.at[0], lr.at[0], at_y(d))

    def l2(k):
        rows = pl.ds(pl.multiple_of(((z + k) % NZ) * PZ, PZ), PZ)
        return remote(part.at[rows], fromz.at[k - 1], ls.at[1], lr.at[1], at_z(k))

    def l3(k, source):
        piece = shb.at[pl.ds(pl.multiple_of(y * PY + source * PZ, PZ), PZ)]
        return remote(piece, piece, ls.at[2], lr.at[2], at_z(k))

    def l4(d, source):
        piece = shb.at[pl.ds(pl.multiple_of(source * PY, PY), PY)]
        return remote(piece, piece, ls.at[3], lr.at[3], at_y(d))

    def adapters_of_tokens():
        eye = lax.broadcasted_iota(jnp.int32, (128, 128), 0) == lax.broadcasted_iota(
            jnp.int32, (128, 128), 1
        )
        upper = (lax.broadcasted_iota(jnp.int32, (128, 128), 1) >= ADAPTER_RANK).astype(jnp.float32)
        ones = jnp.ones((128, 128), jnp.bfloat16)
        for i in range(ROWS // 128):
            row = jnp.broadcast_to(i_ref[pl.ds(i, 1), :].astype(jnp.float32), (128, 128))
            diagonal = jnp.where(eye, row, 0.0).astype(jnp.bfloat16)
            spread = jnp.dot(diagonal, ones, preferred_element_type=jnp.float32)
            idx[pl.ds(i * 128, 128), :] = spread - upper
        acc128[...] = jnp.zeros_like(acc128)

    def shrink_columns(j, carry):
        columns = sv[:, pl.ds(pl.multiple_of(j * 256, 256), 256)]
        first = (4 * j).astype(jnp.float32)
        for r in range(3):
            rows = pl.ds(r * 256, 256)
            out = jnp.dot(fg[0, rows, :], columns, preferred_element_type=jnp.float32)
            which = idx[rows, :]
            acc128[rows, :] += jnp.where(which == first, out[:, :128], 0.0) + jnp.where(
                which == first + 2.0, out[:, 128:], 0.0
            )
        return carry

    def shrink_part(i):
        lax.fori_loop(4 * i, 4 * i + 4, shrink_columns, 0)

    lower = lax.broadcasted_iota(jnp.int32, (96, 128), 1) < ADAPTER_RANK

    def shrink_to_y():
        for r in range(PACKED // 96):
            a = acc128[pl.ds(r * 96, 96), :]
            b = acc128[pl.ds(PACKED + r * 96, 96), :]
            packed[pl.ds(r * 96, 96), :] = jnp.where(
                lower, a + pltpu.roll(a, ADAPTER_RANK, 1), b + pltpu.roll(b, ADAPTER_RANK, 1)
            )
        for d in (2, 1, 3):
            l1(d).start()

    def shrink_to_z():
        received(fromy, lr.at[0])
        part[...] = (
            packed[pl.ds(pl.multiple_of(y * PY, PY), PY), :] + fromy[0] + fromy[1] + fromy[2]
        )
        for k in range(1, NZ):
            @pl.when((z + k) % NZ < ZS)
            def _(k=k):
                l2(k).start()

    def shrunk_to_z():
        @pl.when(z < ZS)
        def _():
            total = part[pl.ds(pl.multiple_of(z * PZ, PZ), PZ), :]
            received(fromz, lr.at[1])
            for k in range(1, NZ):
                total = total + fromz[k - 1]
            shb[pl.ds(pl.multiple_of(y * PY + z * PZ, PZ), PZ), :] = total.astype(jnp.bfloat16)
            for k in range(1, NZ):
                l3(k, z).start()

    def shrunk_to_y():
        @pl.when(z < ZS)
        def _():
            received(shb.at[pl.ds(0, (ZS - 1) * PZ)], lr.at[2])

        @pl.when(z >= ZS)
        def _():
            received(shb.at[pl.ds(0, ZS * PZ)], lr.at[2])

        for d in (2, 1, 3):
            l4(d, y).start()

    def shrunk_here():
        received(shb.at[pl.ds(0, (NY - 1) * PY)], lr.at[3])
        for r in range(PACKED // 96):
            a = shb[pl.ds(r * 96, 96), :].astype(jnp.float32)
            b = pltpu.roll(a, ADAPTER_RANK, 1)
            shr[pl.ds(r * 96, 96), :] = jnp.where(lower, a, b)
            shr[pl.ds(PACKED + r * 96, 96), :] = jnp.where(lower, b, a)

    def expand(i, j):
        n = sum(n for _, n in CHUNKS[i : j + 1])
        rows = pl.ds(CHUNKS[i][0], n)
        which, values = idx[rows, :], shr[rows, :]

        def step(j, total):
            first = (8 * j).astype(jnp.float32)
            wide = jnp.concatenate(
                [jnp.where(which == first + 2.0 * i, values, 0.0).astype(jnp.bfloat16) for i in range(4)],
                axis=1,
            )
            return total + jnp.dot(
                wide, ev[pl.ds(pl.multiple_of(j * 512, 512), 512), :], preferred_element_type=jnp.float32
            )

        o_ref[rows, :] += lax.fori_loop(0, RANKS // 512, step, jnp.zeros((n, COLS), jnp.float32))

    left, right = (x + NX - 1) % NX, (x + 1) % NX

    def from_x(g):
        wx(0, g, left).wait_recv()
        wr(0, g, left).start()
        wx(1, g, right).wait_recv()
        wr(1, g, right).start()

    def from_relay(g):
        s0, n = GROUPS[g]
        received(wg.at[(x + 2) % NX, pl.ds(s0, n), half], wrr.at[g])

    def own(b):
        for d in range(2):
            fc(d, 0, b).start()

    def pass_on(h, b):
        for d in range(2):
            if h <= hops(d, b):
                fc(d, h - 1, b).wait_recv()
            if h < hops(d, b):
                fc(d, h, b).start()

    def from_z(g):
        s0, n = GROUPS[g]
        received(wg.at[x, pl.ds(s0, n), half], wzr.at[g])
        wx(0, g, x).start()
        wx(1, g, x).start()

    def weight_to_z():
        for k in KORD[1:]:
            wz(k).start()
        own_w.wait()
        wx(0, 0, x).start()
        wx(1, 0, x).start()

    def shrink_start():
        adapters_of_tokens()
        own_s.wait()

    def weights_here():
        other = pl.ds(pl.multiple_of((1 - c) * HALF, HALF), HALF)
        received(wg.at[pl.ds(0, NX), pl.ds(0, NZ), other], wcr.at[0])

    def expand_here():
        own_e.wait()
        shrunk_here()

    def product_start(i, j):
        rows = pl.ds(CHUNKS[i][0], sum(n for _, n in CHUNKS[i : j + 1]))
        lhs = jnp.concatenate([fg[s, rows, :] for s in range(NZ - 1)], axis=1)
        for d in range(NY):
            weights = wg[(y + d) % NY, pl.ds(0, NZ - 1)].reshape((NZ - 1) * KD, COLS)
            acc[d, rows, :] = jnp.dot(lhs, weights, preferred_element_type=jnp.float32)

    def product(b):
        rows = rows_of(b)
        lhs = fg[NZ - 1, rows, :]
        for d in (2, 1, 3, 0):
            out = acc[d, rows, :] + jnp.dot(
                lhs, wg[(y + d) % NY, NZ - 1], preferred_element_type=jnp.float32
            )
            if d == 0:
                o_ref[rows, :] = out
            else:
                ys[d - 1, rows, :] = out.astype(jnp.bfloat16)
                yc(d, b).start()

    def finish(b):
        rows = rows_of(b)
        received(yr.at[pl.ds(0, NY - 1), rows], yrs.at[b])
        total = o_ref[rows, :]
        for d in (1, 3, 2):
            total = total + yr[d - 1, rows, :].astype(jnp.float32)
        o_ref[rows, :] = total

    own_f.wait()
    weight_to_z()
    own(0)
    own(1)
    shrink_start()
    shrink_part(0)
    shrink_part(1)
    from_x(0)
    from_z(1)
    shrink_part(2)
    shrink_part(3)
    shrink_to_y()
    from_z(2)
    wc(0, 0, c).start()
    from_x(1)
    from_relay(0)
    from_z(3)
    shrink_to_z()
    from_x(2)
    from_relay(1)
    from_z(4)
    wc(0, 1, c).start()
    wc(1, 0, c).start()
    wc(2, 0, c).start()
    pass_on(1, 0)
    pass_on(1, 1)
    own(2)
    own(3)
    from_x(3)
    from_relay(2)
    wc(3, 0, c).start()
    shrunk_to_z()
    from_x(4)
    wc(1, 1, c).start()
    wc(2, 1, c).start()
    pass_on(2, 0)
    pass_on(2, 1)
    from_relay(3)
    from_relay(4)
    wc(3, 1, c).start()
    shrunk_to_y()
    pass_on(1, 2)
    pass_on(1, 3)
    pass_on(3, 0)
    pass_on(3, 1)
    own(4)
    own(5)
    pass_on(2, 2)
    pass_on(2, 3)
    expand_here()
    pass_on(1, 4)
    pass_on(1, 5)
    weights_here()
    product_start(0, 1)
    pass_on(4, 0)
    pass_on(4, 1)
    product(0)
    product(1)
    pass_on(3, 2)
    pass_on(3, 3)
    pass_on(2, 4)
    pass_on(2, 5)
    product_start(2, 3)
    pass_on(4, 2)
    product(2)
    pass_on(4, 3)
    product(3)
    pass_on(3, 4)
    pass_on(3, 5)
    product_start(4, 5)
    expand(0, 1)
    pass_on(4, 4)
    product(4)
    pass_on(4, 5)
    product(5)
    expand(2, 3)
    expand(4, 5)
    finish(0)
    finish(1)
    finish(2)
    finish(3)
    finish(4)
    finish(5)

    sent(wg.at[0, pl.ds(0, NZ - 1), pl.ds(0, HALF)], wzs.at[0])
    sent(wg.at[pl.ds(0, 2), pl.ds(0, NZ), pl.ds(0, HALF)], wxs.at[0])
    sent(wg.at[0, pl.ds(0, NZ), pl.ds(0, HALF)], wrs.at[0])
    sent(wg.at[pl.ds(0, NX), pl.ds(0, NZ), pl.ds(0, HALF)], wcs.at[0])
    sent(fg.at[pl.ds(0, NZ - 1)], fs.at[0])
    sent(ys, yss.at[0])
    sent(fromy, ls.at[0])

    @pl.when(z < ZS)
    def _():
        sent(part.at[pl.ds(0, (ZS - 1) * PZ)], ls.at[1])
        sent(shb.at[pl.ds(0, (NZ - 1) * PZ)], ls.at[2])

    @pl.when(z >= ZS)
    def _():
        sent(part.at[pl.ds(0, ZS * PZ)], ls.at[1])

    sent(shb.at[pl.ds(0, (NY - 1) * PY)], ls.at[3])


def on_device(features, token_adapter_index, projection_weight, shrink_weight, expand_weight):
    dma = pltpu.SemaphoreType.DMA
    anywhere = pl.BlockSpec(memory_space=pltpu.HBM)
    vmem = pl.BlockSpec(memory_space=pltpu.VMEM)
    return pl.pallas_call(
        kernel,
        out_shape=jax.ShapeDtypeStruct((ROWS, COLS), jnp.float32),
        in_specs=[anywhere, vmem, anywhere, anywhere, anywhere],
        out_specs=vmem,
        scratch_shapes=[
            pltpu.VMEM((NZ, ROWS, KD), jnp.bfloat16),
            pltpu.VMEM((NX, NZ, KD, COLS), jnp.bfloat16),
            pltpu.VMEM((NY - 1, ROWS, COLS), jnp.bfloat16),
            pltpu.VMEM((NY - 1, ROWS, COLS), jnp.bfloat16),
            pltpu.VMEM((KD, RANKS), jnp.bfloat16),
            pltpu.VMEM((RANKS, COLS), jnp.bfloat16),
            pltpu.VMEM((ROWS, 128), jnp.float32),
            pltpu.VMEM((NY, ROWS, COLS), jnp.float32),
            pltpu.VMEM((ROWS, 128), jnp.float32),
            pltpu.VMEM((PACKED, 128), jnp.float32),
            pltpu.VMEM((NY - 1, PY, 128), jnp.float32),
            pltpu.VMEM((PY, 128), jnp.float32),
            pltpu.VMEM((NZ - 1, PZ, 128), jnp.float32),
            pltpu.VMEM((PACKED, 128), jnp.bfloat16),
            pltpu.VMEM((ROWS, 128), jnp.float32),
            dma((4,)),
            dma((1,)), dma((len(GROUPS),)),
            dma((1,)), dma((2, len(GROUPS))),
            dma((1,)), dma((len(GROUPS),)),
            dma((1,)), dma((1,)),
            dma((1,)), dma((2, 4, NB)),
            dma((1,)), dma((NB,)),
            dma((4,)), dma((4,)),
        ],
        compiler_params=pltpu.CompilerParams(
            collective_id=0, has_side_effects=True, vmem_limit_bytes=52 * 1024 * 1024
        ),
        cost_estimate=pl.CostEstimate(
            flops=2 * ROWS * (NZ * KD * NY * COLS + 2 * KD * RANKS),
            bytes_accessed=16 * 1024 * 1024,
            transcendentals=0,
        ),
    )(
        features,
        token_adapter_index.reshape(ROWS // 128, 128),
        projection_weight,
        shrink_weight,
        expand_weight,
    )


def solution(mesh):
    in_specs = (P("dp", "tensor"), P("dp"), P("tensor", None), P("tensor", None), P(None, "tensor"))
    out_specs = P("dp", "tensor")
    return jax.shard_map(
        on_device, mesh=mesh, in_specs=in_specs, out_specs=out_specs, check_vma=False
    )
```

```python
import jax
import jax.numpy as jnp
from jax import lax
from jax.experimental import pallas as pl
from jax.experimental.pallas import tpu as pltpu
from jax.sharding import PartitionSpec as P

ADAPTER_RANK = 64
NX, NC, NY, NZ = 4, 2, 4, 8
ROWS, KD, COLS = 768, 256, 256
RANKS = 4096
PACKED = ROWS // 2
PY = PACKED // NY
PZ = 16
ZS = PY // PZ
CHUNKS = ((0, 128), (128, 128), (256, 128), (384, 128), (512, 128), (640, 128))
NB = len(CHUNKS)


def hops(d, b):
    return 3 + (b + d) % 2


KORD = (0, 1, 7, 2, 6, 3, 5, 4)
SLOT = {k: s for s, k in enumerate(KORD)}
GROUPS = ((0, 1), (1, 2), (3, 2), (5, 2), (7, 1))
GROUP_OF = {KORD[s]: g for g, (s0, n) in enumerate(GROUPS) for s in range(s0, s0 + n)}
HALF = KD // NC
QUART = HALF // 2
def kernel(
    f_ref, i_ref, w_ref, s_ref, e_ref, o_ref,
    fg, wg, ys, yr, sv, ev, idx, acc, acc128, packed, fromy, part, fromz, shb, shr,
    loc, wzs, wzr, wxs, wxr, wrs, wrr, wcs, wcr, fs, fr, yss, yrs,
    ls, lr,
):
    dp, tensor = lax.axis_index("dp"), lax.axis_index("tensor")
    x, c = dp // NC, dp % NC
    y, z = tensor // NZ, tensor % NZ

    def at_z(k):
        return {"tensor": y * NZ + (z + k) % NZ}

    def at_y(d):
        return {"tensor": ((y + d) % NY) * NZ + z}

    def at_x(d):
        return {"dp": ((x + d) % NX) * NC + c}

    sibling = {"dp": x * NC + (1 - c)}

    peers = (
        [at_z(k) for k in range(1, NZ)]
        + [at_y(d) for d in range(1, NY)]
        + [at_x(1), at_x(-1 + NX), sibling]
    )
    barrier = pltpu.get_barrier_semaphore()
    for peer in peers:
        pl.semaphore_signal(barrier, inc=1, device_id=peer, device_id_type=pl.DeviceIdType.MESH)

    own_f = pltpu.make_async_copy(f_ref, fg.at[0], loc.at[0])
    own_f.start()

    def w_part(zz):
        return w_ref.at[
            pl.ds(pl.multiple_of(c * HALF, HALF), HALF),
            pl.ds(pl.multiple_of((x * NZ + zz) * COLS, COLS), COLS),
        ]

    half = pl.ds(pl.multiple_of(c * HALF, HALF), HALF)
    own_w = pltpu.make_async_copy(w_part(z), wg.at[x, 0, half], loc.at[1])
    own_w.start()

    own_s = pltpu.make_async_copy(s_ref, sv, loc.at[2])
    own_s.start()
    own_e = pltpu.make_async_copy(e_ref, ev, loc.at[3])
    own_e.start()

    pl.semaphore_wait(barrier, len(peers))

    def remote(src, dst, s, r, dev):
        return pltpu.make_async_remote_copy(
            src_ref=src, dst_ref=dst, send_sem=s, recv_sem=r,
            device_id=dev, device_id_type=pl.DeviceIdType.MESH,
        )

    def wz(k):
        return remote(
            w_part((z + k) % NZ), wg.at[x, SLOT[k], half], wzs.at[0], wzr.at[GROUP_OF[k]], at_z(k)
        )

    def wx(d, g, owner):
        s0, n = GROUPS[g]
        part = wg.at[owner, pl.ds(s0, n), half]
        return remote(part, part, wxs.at[0], wxr.at[d, g], at_x(1 if d == 0 else NX - 1))

    def wr(d, g, owner):
        s0, n = GROUPS[g]
        rows = pl.ds(pl.multiple_of(c * HALF + d * QUART, QUART), QUART)
        part = wg.at[owner, pl.ds(s0, n), rows]
        return remote(part, part, wrs.at[0], wrr.at[g], at_x(1 if d == 0 else NX - 1))

    def wc(i, h, which):
        owner = (x + (0, NX - 1, 1, 2)[i]) % NX
        part = wg.at[owner, pl.ds(4 * h, 4), pl.ds(pl.multiple_of(which * HALF, HALF), HALF)]
        return remote(part, part, wcs.at[0], wcr.at[0], sibling)

    def rows_of(b):
        return pl.ds(*CHUNKS[b])

    def fc(d, h, b):
        src = SLOT[h] if d == 0 else SLOT[(NZ - h) % NZ]
        dst = SLOT[h + 1] if d == 0 else SLOT[NZ - 1 - h]
        rows = rows_of(b)
        return remote(
            fg.at[src, rows], fg.at[dst, rows], fs.at[0], fr.at[d, h, b], at_z(1 if d == 0 else NZ - 1)
        )

    def yc(d, b):
        rows = rows_of(b)
        return remote(ys.at[d - 1, rows], yr.at[d - 1, rows], yss.at[0], yrs.at[b], at_y(d))

    def sent(ref, sem):
        remote(ref, ref, sem, sem, sibling).wait_send()

    def received(ref, sem):
        remote(ref, ref, sem, sem, sibling).wait_recv()

    def l1(d):
        rows = pl.ds(pl.multiple_of(((y + d) % NY) * PY, PY), PY)
        return remote(packed.at[rows], fromy.at[d - 1], ls.at[0], lr.at[0], at_y(d))

    def l2(k):
        rows = pl.ds(pl.multiple_of(((z + k) % NZ) * PZ, PZ), PZ)
        return remote(part.at[rows], fromz.at[k - 1], ls.at[1], lr.at[1], at_z(k))

    def l3(k, source):
        piece = shb.at[pl.ds(pl.multiple_of(y * PY + source * PZ, PZ), PZ)]
        return remote(piece, piece, ls.at[2], lr.at[2], at_z(k))

    def l4(d, source):
        piece = shb.at[pl.ds(pl.multiple_of(source * PY, PY), PY)]
        return remote(piece, piece, ls.at[3], lr.at[3], at_y(d))

    def adapters_of_tokens():
        eye = lax.broadcasted_iota(jnp.int32, (128, 128), 0) == lax.broadcasted_iota(
            jnp.int32, (128, 128), 1
        )
        upper = (lax.broadcasted_iota(jnp.int32, (128, 128), 1) >= ADAPTER_RANK).astype(jnp.float32)
        ones = jnp.ones((128, 128), jnp.bfloat16)
        for i in range(ROWS // 128):
            row = jnp.broadcast_to(i_ref[pl.ds(i, 1), :].astype(jnp.float32), (128, 128))
            diagonal = jnp.where(eye, row, 0.0).astype(jnp.bfloat16)
            spread = jnp.dot(diagonal, ones, preferred_element_type=jnp.float32)
            idx[pl.ds(i * 128, 128), :] = spread - upper
        acc128[...] = jnp.zeros_like(acc128)

    def shrink_columns(j, carry):
        columns = sv[:, pl.ds(pl.multiple_of(j * 256, 256), 256)]
        first = (4 * j).astype(jnp.float32)
        for r in range(3):
            rows = pl.ds(r * 256, 256)
            out = jnp.dot(fg[0, rows, :], columns, preferred_element_type=jnp.float32)
            which = idx[rows, :]
            acc128[rows, :] += jnp.where(which == first, out[:, :128], 0.0) + jnp.where(
                which == first + 2.0, out[:, 128:], 0.0
            )
        return carry

    def shrink_part(i):
        lax.fori_loop(4 * i, 4 * i + 4, shrink_columns, 0)

    lower = lax.broadcasted_iota(jnp.int32, (96, 128), 1) < ADAPTER_RANK

    def shrink_to_y():
        for r in range(PACKED // 96):
            a = acc128[pl.ds(r * 96, 96), :]
            b = acc128[pl.ds(PACKED + r * 96, 96), :]
            packed[pl.ds(r * 96, 96), :] = jnp.where(
                lower, a + pltpu.roll(a, ADAPTER_RANK, 1), b + pltpu.roll(b, ADAPTER_RANK, 1)
            )
        for d in (2, 1, 3):
            l1(d).start()

    def shrink_to_z():
        received(fromy, lr.at[0])
        part[...] = (
            packed[pl.ds(pl.multiple_of(y * PY, PY), PY), :] + fromy[0] + fromy[1] + fromy[2]
        )
        for k in range(1, NZ):
            @pl.when((z + k) % NZ < ZS)
            def _(k=k):
                l2(k).start()

    def shrunk_to_z():
        @pl.when(z < ZS)
        def _():
            total = part[pl.ds(pl.multiple_of(z * PZ, PZ), PZ), :]
            received(fromz, lr.at[1])
            for k in range(1, NZ):
                total = total + fromz[k - 1]
            shb[pl.ds(pl.multiple_of(y * PY + z * PZ, PZ), PZ), :] = total.astype(jnp.bfloat16)
            for k in range(1, NZ):
                l3(k, z).start()

    def shrunk_to_y():
        @pl.when(z < ZS)
        def _():
            received(shb.at[pl.ds(0, (ZS - 1) * PZ)], lr.at[2])

        @pl.when(z >= ZS)
        def _():
            received(shb.at[pl.ds(0, ZS * PZ)], lr.at[2])

        for d in (2, 1, 3):
            l4(d, y).start()

    def shrunk_here():
        received(shb.at[pl.ds(0, (NY - 1) * PY)], lr.at[3])
        for r in range(PACKED // 96):
            a = shb[pl.ds(r * 96, 96), :].astype(jnp.float32)
            b = pltpu.roll(a, ADAPTER_RANK, 1)
            shr[pl.ds(r * 96, 96), :] = jnp.where(lower, a, b)
            shr[pl.ds(PACKED + r * 96, 96), :] = jnp.where(lower, b, a)

    def expand(i, j):
        n = sum(n for _, n in CHUNKS[i : j + 1])
        rows = pl.ds(CHUNKS[i][0], n)
        which, values = idx[rows, :], shr[rows, :]

        def step(j, total):
            first = (8 * j).astype(jnp.float32)
            wide = jnp.concatenate(
                [jnp.where(which == first + 2.0 * i, values, 0.0).astype(jnp.bfloat16) for i in range(4)],
                axis=1,
            )
            return total + jnp.dot(
                wide, ev[pl.ds(pl.multiple_of(j * 512, 512), 512), :], preferred_element_type=jnp.float32
            )

        o_ref[rows, :] += lax.fori_loop(0, RANKS // 512, step, jnp.zeros((n, COLS), jnp.float32))

    left, right = (x + NX - 1) % NX, (x + 1) % NX

    def from_x(g):
        wx(0, g, left).wait_recv()
        wr(0, g, left).start()
        wx(1, g, right).wait_recv()
        wr(1, g, right).start()

    def from_relay(g):
        s0, n = GROUPS[g]
        received(wg.at[(x + 2) % NX, pl.ds(s0, n), half], wrr.at[g])

    def own(b):
        for d in range(2):
            fc(d, 0, b).start()

    def pass_on(h, b):
        for d in range(2):
            if h <= hops(d, b):
                fc(d, h - 1, b).wait_recv()
            if h < hops(d, b):
                fc(d, h, b).start()

    def from_z(g):
        s0, n = GROUPS[g]
        received(wg.at[x, pl.ds(s0, n), half], wzr.at[g])
        wx(0, g, x).start()
        wx(1, g, x).start()

    def weight_to_z():
        for k in KORD[1:]:
            wz(k).start()
        own_w.wait()
        wx(0, 0, x).start()
        wx(1, 0, x).start()

    def shrink_start():
        adapters_of_tokens()
        own_s.wait()

    def weights_here():
        other = pl.ds(pl.multiple_of((1 - c) * HALF, HALF), HALF)
        received(wg.at[pl.ds(0, NX), pl.ds(0, NZ), other], wcr.at[0])

    def expand_here():
        own_e.wait()
        shrunk_here()

    def product_start(i, j):
        rows = pl.ds(CHUNKS[i][0], sum(n for _, n in CHUNKS[i : j + 1]))
        lhs = jnp.concatenate([fg[s, rows, :] for s in range(NZ - 1)], axis=1)
        for d in range(NY):
            weights = wg[(y + d) % NY, pl.ds(0, NZ - 1)].reshape((NZ - 1) * KD, COLS)
            acc[d, rows, :] = jnp.dot(lhs, weights, preferred_element_type=jnp.float32)

    def product(b):
        rows = rows_of(b)
        lhs = fg[NZ - 1, rows, :]
        for d in (2, 1, 3, 0):
            out = acc[d, rows, :] + jnp.dot(
                lhs, wg[(y + d) % NY, NZ - 1], preferred_element_type=jnp.float32
            )
            if d == 0:
                o_ref[rows, :] = out
            else:
                ys[d - 1, rows, :] = out.astype(jnp.bfloat16)
                yc(d, b).start()

    def finish(b):
        rows = rows_of(b)
        received(yr.at[pl.ds(0, NY - 1), rows], yrs.at[b])
        total = o_ref[rows, :]
        for d in (1, 3, 2):
            total = total + yr[d - 1, rows, :].astype(jnp.float32)
        o_ref[rows, :] = total

    own_f.wait()
    weight_to_z()
    own(0)
    own(1)
    shrink_start()
    shrink_part(0)
    shrink_part(1)
    from_x(0)
    from_z(1)
    shrink_part(2)
    shrink_part(3)
    shrink_to_y()
    from_z(2)
    wc(0, 0, c).start()
    from_x(1)
    from_relay(0)
    from_z(3)
    from_x(2)
    from_relay(1)
    from_z(4)
    wc(0, 1, c).start()
    wc(1, 0, c).start()
    wc(2, 0, c).start()
    pass_on(1, 0)
    pass_on(1, 1)
    own(2)
    own(3)
    from_x(3)
    from_relay(2)
    wc(3, 0, c).start()
    shrink_to_z()
    from_x(4)
    wc(1, 1, c).start()
    wc(2, 1, c).start()
    pass_on(2, 0)
    pass_on(2, 1)
    from_relay(3)
    from_relay(4)
    wc(3, 1, c).start()
    pass_on(1, 2)
    pass_on(1, 3)
    shrunk_to_z()
    pass_on(3, 0)
    pass_on(3, 1)
    own(4)
    own(5)
    weights_here()
    product_start(0, 1)
    pass_on(2, 2)
    pass_on(2, 3)
    pass_on(4, 0)
    pass_on(4, 1)
    product(0)
    product(1)
    pass_on(1, 4)
    pass_on(1, 5)
    shrunk_to_y()
    pass_on(3, 2)
    pass_on(3, 3)
    pass_on(2, 4)
    pass_on(2, 5)
    product_start(2, 3)
    pass_on(4, 2)
    product(2)
    pass_on(4, 3)
    product(3)
    pass_on(3, 4)
    pass_on(3, 5)
    product_start(4, 5)
    pass_on(4, 4)
    product(4)
    pass_on(4, 5)
    product(5)
    expand_here()
    expand(0, 1)
    expand(2, 3)
    expand(4, 5)
    finish(0)
    finish(1)
    finish(2)
    finish(3)
    finish(4)
    finish(5)

    sent(wg.at[0, pl.ds(0, NZ - 1), pl.ds(0, HALF)], wzs.at[0])
    sent(wg.at[pl.ds(0, 2), pl.ds(0, NZ), pl.ds(0, HALF)], wxs.at[0])
    sent(wg.at[0, pl.ds(0, NZ), pl.ds(0, HALF)], wrs.at[0])
    sent(wg.at[pl.ds(0, NX), pl.ds(0, NZ), pl.ds(0, HALF)], wcs.at[0])
    sent(fg.at[pl.ds(0, NZ - 1)], fs.at[0])
    sent(ys, yss.at[0])
    sent(fromy, ls.at[0])

    @pl.when(z < ZS)
    def _():
        sent(part.at[pl.ds(0, (ZS - 1) * PZ)], ls.at[1])
        sent(shb.at[pl.ds(0, (NZ - 1) * PZ)], ls.at[2])

    @pl.when(z >= ZS)
    def _():
        sent(part.at[pl.ds(0, ZS * PZ)], ls.at[1])

    sent(shb.at[pl.ds(0, (NY - 1) * PY)], ls.at[3])


def on_device(features, token_adapter_index, projection_weight, shrink_weight, expand_weight):
    dma = pltpu.SemaphoreType.DMA
    anywhere = pl.BlockSpec(memory_space=pltpu.HBM)
    vmem = pl.BlockSpec(memory_space=pltpu.VMEM)
    return pl.pallas_call(
        kernel,
        out_shape=jax.ShapeDtypeStruct((ROWS, COLS), jnp.float32),
        in_specs=[anywhere, vmem, anywhere, anywhere, anywhere],
        out_specs=vmem,
        scratch_shapes=[
            pltpu.VMEM((NZ, ROWS, KD), jnp.bfloat16),
            pltpu.VMEM((NX, NZ, KD, COLS), jnp.bfloat16),
            pltpu.VMEM((NY - 1, ROWS, COLS), jnp.bfloat16),
            pltpu.VMEM((NY - 1, ROWS, COLS), jnp.bfloat16),
            pltpu.VMEM((KD, RANKS), jnp.bfloat16),
            pltpu.VMEM((RANKS, COLS), jnp.bfloat16),
            pltpu.VMEM((ROWS, 128), jnp.float32),
            pltpu.VMEM((NY, ROWS, COLS), jnp.float32),
            pltpu.VMEM((ROWS, 128), jnp.float32),
            pltpu.VMEM((PACKED, 128), jnp.float32),
            pltpu.VMEM((NY - 1, PY, 128), jnp.float32),
            pltpu.VMEM((PY, 128), jnp.float32),
            pltpu.VMEM((NZ - 1, PZ, 128), jnp.float32),
            pltpu.VMEM((PACKED, 128), jnp.bfloat16),
            pltpu.VMEM((ROWS, 128), jnp.float32),
            dma((4,)),
            dma((1,)), dma((len(GROUPS),)),
            dma((1,)), dma((2, len(GROUPS))),
            dma((1,)), dma((len(GROUPS),)),
            dma((1,)), dma((1,)),
            dma((1,)), dma((2, 4, NB)),
            dma((1,)), dma((NB,)),
            dma((4,)), dma((4,)),
        ],
        compiler_params=pltpu.CompilerParams(
            collective_id=0, has_side_effects=True, vmem_limit_bytes=52 * 1024 * 1024
        ),
        cost_estimate=pl.CostEstimate(
            flops=2 * ROWS * (NZ * KD * NY * COLS + 2 * KD * RANKS),
            bytes_accessed=16 * 1024 * 1024,
            transcendentals=0,
        ),
    )(
        features,
        token_adapter_index.reshape(ROWS // 128, 128),
        projection_weight,
        shrink_weight,
        expand_weight,
    )


def solution(mesh):
    in_specs = (P("dp", "tensor"), P("dp"), P("tensor", None), P("tensor", None), P(None, "tensor"))
    out_specs = P("dp", "tensor")
    return jax.shard_map(
        on_device, mesh=mesh, in_specs=in_specs, out_specs=out_specs, check_vma=False
    )
```
